32 devices in a mesh: clu: 8 (over z, y), rhs: 4 (over x, core).
Axes of the slice: x: 2, y: 2, z: 4, core: 2. Of those that a mesh axis runs over, the one named last changes fastest.
Arguments:
- right_side: float32 [64, 4096], P('rhs', 'clu')
- self_term: float32 [4096], P('clu'), may hold values from 3 to 9
- near_pairs: int32 [512, 2], P('clu'), may hold values from 0 to 15, as said below
- near_blocks: bfloat16 [512, 256, 256], P('clu'), may hold values from -0.046875 to 0.046875
- near_scale: float32 [512], P('clu'), may hold values from 0.5 to 1.5
- near_count: int32 [8], P('clu'), may hold values from 16 to 64, as said below
- far_pairs: int32 [512, 2], P('clu'), may hold values from 0 to 15, as said below
- far_left: bfloat16 [512, 32, 256], P('clu'), may hold values from -1 to 1
- far_right: bfloat16 [512, 32, 256], P('clu'), may hold values from -1 to 1
- far_scale: float32 [512], P('clu'), may hold values from 0.03 to 0.1
- far_rank: int32 [512], P('clu'), may hold values from 8 to 32, as said below
- far_count: int32 [8], P('clu'), may hold values from 16 to 64, as said below
Outputs:
- solution: float32 [64, 4096], P('rhs', 'clu')
- residual: float32 [64, 4096], P('rhs', 'clu')
The draws below stay inside these ranges and needn't reach their ends.
Inputs may be any that keep to these rules, and one draw needn't show every extreme that they name: near_pairs[s, 0] is one of the 2 clusters of the index of clu that holds slot s (s // 64); near_pairs[s, 1] is a cluster of that index or of the index beside it on either side. far_pairs[s, 0] is one of the 2 clusters of the index of clu that holds slot s (s // 64); among the slots of one index of clu, at most 16 have their second cluster on any one index of clu, and some index of clu holds the second cluster of exactly 16 slots of every index. `near_count`: live near slots of each index of clu; slots at or after the count hold blocks that are ignored. `far_count`: live far slots of each index of clu; slots at or after the count hold blocks that are ignored. Only the first far_rank rows of a far block's factors are used.
All inputs are finite; a program needn't handle non-finite values.
Results may differ from the reference program's by a relative error of at most 0.0019.
Values may be sent and summed in bfloat16 or wider, within the bound.
A program may use at most 64 MiB of HBM per device.

```python
import math
import jax
import jax.numpy as jnp
from jax import lax

CLUSTER = 256
CL_DEV = 2
RHS = 64
RANK = 32
NEAR_DEV = 64
FAR_DEV = 64
ITERS = 2
NCL = 16
NP = 4096
NEAR_ALL = 512
FAR_ALL = 512
FAR_CAP = 16


def capped_counts(key, length, lowest, highest):
    first_key, second_key = jax.random.split(key)
    counts = jax.random.randint(first_key, (length,), lowest, highest + 1)
    busiest = jax.random.randint(second_key, (), 0, length)
    return jnp.where(jnp.arange(length) == busiest, highest, counts).astype(jnp.int32)


def draw_right_side(key, part):
    key = jax.random.fold_in(key, 11)
    base_key, rough_key = jax.random.split(key, 2)
    position = jnp.arange(NP, dtype=jnp.float32) / NP
    rising = jnp.exp(jnp.log(3.0) * position)
    rough = jax.random.uniform(rough_key, (NP,), minval=0.5, maxval=1.5)
    base = jnp.clip(jax.random.normal(base_key, (RHS, NP)), -4.0, 4.0)
    return (base * rising[None, :] * rough[None, :]).astype(jnp.float32)


def draw_near_pairs(key, part):
    key = jax.random.fold_in(key, 47)
    first_key, second_key = jax.random.split(key)
    holder = jnp.arange(NEAR_ALL, dtype=jnp.int32) // NEAR_DEV
    first = holder * CL_DEV + jax.random.randint(first_key, (NEAR_ALL,), 0, CL_DEV)
    second = holder * CL_DEV + jax.random.randint(second_key, (NEAR_ALL,), -CL_DEV, 2 * CL_DEV)
    second = jnp.clip(second, 0, NCL - 1)
    return jnp.stack([first, second], axis=1).astype(jnp.int32)


def draw_far_pairs(key, part):
    key = jax.random.fold_in(key, 53)
    first_key, second_key, seat_key, star_key = jax.random.split(key, 4)
    holders = FAR_ALL // FAR_DEV
    seat_total = holders * FAR_CAP
    star = jax.random.randint(star_key, (), 0, holders)
    seat_ids = jnp.arange(seat_total, dtype=jnp.int32)

    def order_for(sub_key):
        shuffled = jax.random.permutation(sub_key, seat_total).astype(jnp.int32)
        score = jnp.where(seat_ids // FAR_CAP == star, seat_ids % FAR_CAP - FAR_CAP, shuffled)
        return jnp.argsort(score, stable=True)[:FAR_DEV]
    orders = jax.vmap(order_for)(jax.random.split(seat_key, holders))
    target = (orders // FAR_CAP).reshape(FAR_ALL).astype(jnp.int32)
    holder = jnp.arange(FAR_ALL, dtype=jnp.int32) // FAR_DEV
    first = holder * CL_DEV + jax.random.randint(first_key, (FAR_ALL,), 0, CL_DEV)
    second = target * CL_DEV + jax.random.randint(second_key, (FAR_ALL,), 0, CL_DEV)
    return jnp.stack([first, second], axis=1).astype(jnp.int32)


def draw_near_count(key, part):
    key = jax.random.fold_in(key, 23)
    return capped_counts(key, NEAR_ALL // NEAR_DEV, NEAR_DEV // 4, NEAR_DEV)


def draw_far_count(key, part):
    key = jax.random.fold_in(key, 37)
    return capped_counts(key, FAR_ALL // FAR_DEV, FAR_DEV // 4, FAR_DEV)


def draw_far_rank(key, part):
    key = jax.random.fold_in(key, 41)
    return capped_counts(key, FAR_ALL, RANK // 4, RANK)


def block_scale(rng, shape, shards, least, largest):
    gain = 1.0
    for axis_at, blocks in shards:
        draws = jax.random.uniform(jax.random.fold_in(jax.random.fold_in(rng, 6), axis_at), (blocks,), jnp.float32, least / len(shards), largest / len(shards))
        gain = gain * jnp.repeat(jnp.exp(draws), shape[axis_at] // blocks).reshape((-1,) + (1,) * (len(shape) - 1 - axis_at))
    return gain


def bell_draw(stream_key, dims, scale, bound, pieces=(), kind=jnp.bfloat16):
    array = jax.random.normal(stream_key, dims, jnp.float32) * scale
    if len(pieces) > 0:
        array = block_scale(stream_key, dims, pieces, -0.22, 0.18) * array
    return jnp.clip(array, min=-bound, max=bound).astype(kind)


def setup_inputs(seed: int = 0) -> dict:
    key_of = jax.random.split(jax.random.key(seed), 13)
    right_side = draw_right_side(jax.random.fold_in(key_of[12], 71), 0)
    self_term = jnp.clip(jnp.exp(math.log(9.0) - 1.0986123 * jax.random.uniform(key_of[1], (NP,), jnp.float32) ** block_scale(key_of[1], (NP,), ((0, 8),), -0.2, 0.2)), 3.0, 9.0)
    near_pairs = draw_near_pairs(jax.random.fold_in(key_of[12], 71), 0)
    near_blocks = bell_draw(key_of[3], (NEAR_ALL, CLUSTER, CLUSTER), (0.1 / (2 * CLUSTER ** 0.5)), 0.046875, ((0, 8),))
    near_scale = jnp.clip(jnp.exp(math.log(1.5) - 1.0986123 * jax.random.uniform(key_of[4], (NEAR_ALL,), jnp.float32) ** block_scale(key_of[4], (NEAR_ALL,), ((0, 8),), -0.2, 0.2)), 0.5, 1.5)
    near_count = draw_near_count(jax.random.fold_in(key_of[12], 71), 0)
    far_pairs = draw_far_pairs(jax.random.fold_in(key_of[12], 71), 0)
    far_left = bell_draw(key_of[7], (FAR_ALL, RANK, CLUSTER), (1 / CLUSTER ** 0.5), 1.0, ((0, 8),))
    far_right = bell_draw(key_of[8], (FAR_ALL, RANK, CLUSTER), (1 / CLUSTER ** 0.5), 1.0, ((0, 8),))
    far_scale = jnp.clip(jnp.exp(math.log(0.1) - 1.2039728 * jax.random.uniform(key_of[9], (FAR_ALL,), jnp.float32) ** block_scale(key_of[9], (FAR_ALL,), ((0, 8),), -0.2, 0.2)), 0.03, 0.1)
    far_rank = draw_far_rank(jax.random.fold_in(key_of[12], 71), 0)
    far_count = draw_far_count(jax.random.fold_in(key_of[12], 71), 0)
    return {"right_side": right_side, "self_term": self_term, "near_pairs": near_pairs, "near_blocks": near_blocks, "near_scale": near_scale, "near_count": near_count, "far_pairs": far_pairs, "far_left": far_left, "far_right": far_right, "far_scale": far_scale, "far_rank": far_rank, "far_count": far_count}


def apply_operator(charge_field, self_term, near_pairs, near_blocks, near_scale, near_count, far_pairs, far_left, far_right, far_scale, far_rank, far_count):
    charges = charge_field.astype(jnp.bfloat16).reshape(RHS, NCL, CLUSTER)
    near_slots = jnp.arange(NEAR_ALL, dtype=jnp.int32)
    near_live = (near_slots % NEAR_DEV < near_count[near_slots // NEAR_DEV]).astype(jnp.float32)
    near_weight = near_scale * near_live
    far_slots = jnp.arange(FAR_ALL, dtype=jnp.int32)
    far_live = (far_slots % FAR_DEV < far_count[far_slots // FAR_DEV]).astype(jnp.float32)
    far_weight = far_scale * far_live

    def near_step(summed, item):
        pair, block, weight = item
        first_cl = pair[0]
        second_cl = pair[1]
        toward_first = jnp.dot(charges[:, second_cl].astype(jnp.float32), block.T.astype(jnp.float32), preferred_element_type=jnp.float32)
        toward_second = jnp.dot(charges[:, first_cl].astype(jnp.float32), block.astype(jnp.float32), preferred_element_type=jnp.float32)
        summed = summed.at[:, first_cl].add(weight * toward_first)
        summed = summed.at[:, second_cl].add(weight * toward_second)
        return (summed, None)

    def far_step(summed, item):
        pair, left_factor, right_factor, weight, rank_used = item
        first_cl = pair[0]
        second_cl = pair[1]
        keeps = jnp.arange(RANK, dtype=jnp.int32) < rank_used
        coef_second = jnp.dot(charges[:, second_cl].astype(jnp.float32), right_factor.T.astype(jnp.float32), preferred_element_type=jnp.float32)
        coef_second = jnp.where(keeps[None, :], coef_second, 0.0).astype(jnp.bfloat16)
        coef_first = weight * jnp.dot(charges[:, first_cl].astype(jnp.float32), left_factor.T.astype(jnp.float32), preferred_element_type=jnp.float32)
        coef_first = jnp.where(keeps[None, :], coef_first, 0.0).astype(jnp.bfloat16)
        toward_first = weight * jnp.dot(coef_second.astype(jnp.float32), left_factor.astype(jnp.float32), preferred_element_type=jnp.float32)
        toward_second = jnp.dot(coef_first.astype(jnp.float32), right_factor.astype(jnp.float32), preferred_element_type=jnp.float32)
        summed = summed.at[:, first_cl].add(toward_first)
        summed = summed.at[:, second_cl].add(toward_second)
        return (summed, None)
    summed = jnp.zeros((RHS, NCL, CLUSTER), jnp.float32)
    summed, _ = lax.scan(near_step, summed, (near_pairs, near_blocks, near_weight))
    summed, _ = lax.scan(far_step, summed, (far_pairs, far_left, far_right, far_weight, far_rank))
    return self_term[None, :] * charge_field + summed.reshape(RHS, NP)

def solve_spd(matrix, target):
    return jax.scipy.linalg.cho_solve((jnp.linalg.cholesky(matrix), True), target)

def reference(right_side, self_term, near_pairs, near_blocks, near_scale, near_count, far_pairs, far_left, far_right, far_scale, far_rank, far_count):
    precise = lax.Precision.HIGHEST
    solution = jnp.zeros_like(right_side)
    residual = right_side
    direction = right_side
    norms = jnp.dot(residual, residual.T, precision=precise)
    for step in range(ITERS):
        image = apply_operator(direction, self_term, near_pairs, near_blocks, near_scale, near_count, far_pairs, far_left, far_right, far_scale, far_rank, far_count)
        curvature = jnp.dot(direction, image.T, precision=precise)
        alpha = solve_spd(curvature, norms)
        solution = solution + jnp.dot(alpha.T, direction, precision=precise)
        residual = residual - jnp.dot(alpha.T, image, precision=precise)
        if step + 1 < ITERS:
            norms_next = jnp.dot(residual, residual.T, precision=precise)
            beta = solve_spd(norms, norms_next)
            direction = residual + jnp.dot(beta.T, direction, precision=precise)
            norms = norms_next
    return (solution, residual)
```

```python
import functools

import jax
import jax.numpy as jnp
from jax import lax
from jax.experimental import pallas as pl
from jax.experimental.pallas import tpu as pltpu
from jax.sharding import PartitionSpec as P

CLUSTER = 256
PRECISE = lax.Precision.HIGHEST
F32 = jnp.float32
BF16 = jnp.bfloat16
MESH = pl.DeviceIdType.MESH

NT = (((1,), (1,)), ((), ()))
NN = (((1,), (0,)), ((), ()))
TN = (((0,), (0,)), ((), ()))


def dot(left, right, dims):
    return lax.dot_general(left, right, dims, preferred_element_type=F32)


def exact(left, right, dims):
    return lax.dot_general(left, right, dims, precision=PRECISE, preferred_element_type=F32)


def solve_many(systems):
    size, wide = systems[0].shape
    step = 8
    row_at = lax.broadcasted_iota(jnp.int32, (size, 1), 0)

    def block(_, current):
        current = list(current)
        for k in range(step):
            for at, m in enumerate(current):
                column = m[:, k : k + 1]
                row = m[k : k + 1, :] * (1.0 / m[k : k + 1, k : k + 1])
                current[at] = jnp.where(row_at == k, row, m - column * row)
        return tuple(
            pltpu.roll(jnp.concatenate([m[step:], m[:step]], axis=0), wide - step, 1)
            for m in current
        )

    done = lax.fori_loop(0, size // step, block, tuple(systems))
    return [m[:, : wide - size] for m in done]


def kernel(
    sizes,
    right_ref,
    self_ref,
    near_pairs,
    near_scale,
    near_count,
    far_pairs,
    far_scale,
    far_rank,
    far_count,
    near_hbm,
    left_hbm,
    rightf_hbm,
    solution_ref,
    residual_ref,
    near,
    far_l,
    far_r,
    meta_i,
    meta_j,
    meta_keep,
    meta_w,
    lhs,
    grid,
    around,
    sums,
    parts,
    slabs,
    all_right,
    all_image,
    all_direction,
    all_residual,
    grams,
    first_solution,
    load_sem,
    clu_send,
    clu_recv,
    rhs_send,
    rhs_recv,
):
    n_clu, n_rhs, rows, near_slots, far_slots, rank = sizes
    me, col = lax.axis_index("clu"), lax.axis_index("rhs")
    n_cl = 2 * n_clu
    own = pl.ds(pl.multiple_of(col * rows, rows), rows)
    own_block = pl.ds(pl.multiple_of(me * 2 * rows, 2 * rows), 2 * rows)
    tile = 256
    slots_tile = tile // rank
    tiles = far_slots // slots_tile
    group = 4

    def near_load(g):
        part = pl.ds(g * (near_slots // group), near_slots // group)
        return pltpu.make_async_copy(near_hbm.at[part], near.at[part], load_sem.at[2 + g])

    loads = [
        pltpu.make_async_copy(left_hbm, far_l, load_sem.at[0]),
        pltpu.make_async_copy(rightf_hbm, far_r, load_sem.at[1]),
    ] + [near_load(g) for g in range(group)]
    for load in loads:
        load.start()

    barrier = pltpu.get_barrier_semaphore()

    @pl.loop(1, n_clu)
    def _(d):
        pl.semaphore_signal(
            barrier, inc=1, device_id={"clu": lax.rem(me + d, n_clu)}, device_id_type=MESH
        )

    for d in range(1, n_rhs):
        pl.semaphore_signal(
            barrier, inc=1, device_id={"rhs": lax.rem(col + d, n_rhs)}, device_id_type=MESH
        )

    def clu_copy(kind, d, src, dst):
        return pltpu.make_async_remote_copy(
            src_ref=src,
            dst_ref=dst,
            send_sem=clu_send.at[kind, d],
            recv_sem=clu_recv.at[kind, d],
            device_id={"clu": lax.rem(me + d, n_clu)},
            device_id_type=MESH,
        )

    def rhs_copy(kind, d, ref):
        return pltpu.make_async_remote_copy(
            src_ref=ref.at[own],
            dst_ref=ref.at[own],
            send_sem=rhs_send.at[kind, d],
            recv_sem=rhs_recv.at[kind, d],
            device_id={"rhs": lax.rem(col + d, n_rhs)},
            device_id_type=MESH,
        )

    def rhs_start(kind, ref):
        for d in range(1, n_rhs):
            rhs_copy(kind, d, ref).start()

    def rhs_wait(kind, ref):
        for d in range(1, n_rhs):
            rhs_copy(kind, d, ref).wait()

    def grid_copy(it, d):
        block = grid.at[it, own_block]
        return clu_copy(it, d, block, block)

    def slab_copy(which, d):
        block = slabs.at[which, me]
        return clu_copy(4 + which, d, block, block)

    def sums_copy(it, d):
        there = lax.rem(me + d, n_clu)
        src = sums.at[it, pl.ds(pl.multiple_of(there * 2 * rows, 2 * rows), 2 * rows)]
        return clu_copy(2 + it, d, src, parts.at[it, me])

    def start_all(copy, which):
        @pl.loop(1, n_clu)
        def _(d):
            copy(which, d).start()

    def wait_all(copy, which):
        @pl.loop(1, n_clu)
        def _(d):
            copy(which, d).wait()

    def set_charges(it, field):
        grid[it, own_block] = jnp.concatenate(
            [field[:, :CLUSTER], field[:, CLUSTER:]], axis=0
        ).astype(BF16)

    def slab_sum(which):
        return lax.fori_loop(
            1, n_clu, lambda k, total: total + slabs[which, k], slabs[which, 0]
        )

    field = right_ref[...]
    set_charges(0, field)
    all_right[own] = field
    pl.semaphore_wait(barrier, n_clu + n_rhs - 2)
    start_all(grid_copy, 0)
    rhs_start(0, all_right)

    lane = lax.broadcasted_iota(jnp.int32, (1, 128), 1)
    slot_in = lane // rank
    live = far_count[0]
    per = 128 // rank
    for g in range(far_slots // per):
        at = slice(g * 128, (g + 1) * 128)

        def spread(value):
            out = jnp.full((1, 128), value(g * per))
            for q in range(1, per):
                out = jnp.where(slot_in == q, value(g * per + q), out)
            return out

        meta_i[:, at] = spread(lambda s: far_pairs[s, 0])
        meta_j[:, at] = spread(lambda s: far_pairs[s, 1])
        meta_keep[:, at] = jnp.where(
            lane - slot_in * rank < spread(lambda s: far_rank[s]), 1.0, 0.0
        )
        meta_w[:, at] = spread(
            lambda s: jnp.where(s < live, far_scale[s], jnp.zeros((), F32))
        )

    rhs_wait(0, all_right)
    blank = jnp.zeros((rows, 128 - n_rhs * rows), F32)
    slabs[0, me] = jnp.concatenate([exact(all_right[own], all_right[...], NT), blank], axis=1)
    start_all(slab_copy, 0)

    def apply(it, field):
        first_far = jnp.zeros((4 * rows, CLUSTER), F32)
        for t in range(tiles):
            at = slice(t * tile, (t + 1) * tile)
            right_tile, left_tile = far_r[at, :], far_l[at, :]
            to_i, to_j = meta_i[:, at], meta_j[:, at]
            keep, weight = meta_keep[:, at], meta_w[:, at]

            def pick(b, coef):
                base = pl.multiple_of(b * 16 * rows, 16 * rows)
                product = dot(grid[it, pl.ds(base, 16 * rows)], right_tile, NT)
                for q in range(16):
                    coef = coef + jnp.where(
                        to_j == b * 16 + q, product[q * rows : (q + 1) * rows], 0.0
                    )
                return coef

            coef_second = jnp.zeros((rows, tile), F32)
            if n_cl == 16:
                coef_second = pick(0, coef_second)
            else:
                coef_second = lax.fori_loop(0, n_cl // 16, pick, coef_second)
            coef_second = jnp.where(keep > 0.0, coef_second, 0.0).astype(BF16).astype(F32) * weight
            high = coef_second.astype(BF16).astype(F32)
            low = coef_second - high
            low_cluster = to_i == 2 * me
            stack = jnp.concatenate(
                [
                    jnp.where(low_cluster, high, 0.0),
                    jnp.where(low_cluster, 0.0, high),
                    jnp.where(low_cluster, low, 0.0),
                    jnp.where(low_cluster, 0.0, low),
                ],
                axis=0,
            ).astype(BF16)
            first_far = first_far + dot(stack, left_tile, NN)
            both = dot(grid[it, own_block], left_tile, NT)
            coef_first = jnp.where(low_cluster, both[:rows], both[rows:]) * weight
            coef_first = jnp.where(keep > 0.0, coef_first, 0.0)

            def spread_rows(b, carry):
                for q in range(16):
                    base = pl.multiple_of(b * 16 * rows + q * rows, rows)
                    lhs[pl.ds(base, rows), at] = jnp.where(
                        to_j == b * 16 + q, coef_first, 0.0
                    ).astype(BF16)
                return carry

            if n_cl == 16:
                spread_rows(0, 0)
            else:
                lax.fori_loop(0, n_cl // 16, spread_rows, 0)

        def second_far(b, carry):
            part = pl.ds(pl.multiple_of(b * 16 * rows, 16 * rows), 16 * rows)
            sums[it, part] = dot(lhs[part], far_r[...], NN)
            return carry

        lax.fori_loop(0, n_cl // 16, second_far, 0)

        @pl.loop(2, n_clu - 1)
        def _(d):
            sums_copy(it, d).start()

        for side, there in enumerate((me + n_clu - 1, me, me + 1)):
            base = pl.multiple_of(lax.rem(there, n_clu) * 2 * rows, 2 * rows)
            around[side * 2 * rows : (side + 1) * 2 * rows] = grid[
                it, pl.ds(base, 2 * rows)
            ].astype(F32)
        near_live = near_count[0]
        unroll = 4
        zero = jnp.zeros((rows, CLUSTER), F32)

        def near_slots_step(g, carry):
            carry = list(carry)
            for u in range(unroll):
                s = g * unroll + u
                i, j = near_pairs[s, 0], near_pairs[s, 1]
                weight = jnp.where(s < near_live, near_scale[s], jnp.zeros((), F32))
                block = near[s]
                offset = j - 2 * me + 2
                offset = jnp.where(offset < 0, offset + n_cl, offset)
                offset = jnp.where(offset >= n_cl, offset - n_cl, offset)
                is_first = [jnp.where(i - 2 * me == q, 1.0, 0.0) for q in range(2)]
                is_second = [jnp.where(offset == q, 1.0, 0.0) for q in range(6)]
                first = is_first[0] * around[2 * rows : 3 * rows]
                first = first + is_first[1] * around[3 * rows : 4 * rows]
                second = is_second[0] * around[:rows]
                for q in range(1, 6):
                    second = second + is_second[q] * around[q * rows : (q + 1) * rows]
                toward_first = dot(second.astype(BF16), block, NT)
                toward_second = dot(first.astype(BF16), block, NN)
                for q in range(2):
                    carry[q] = carry[q] + (is_first[q] * weight) * toward_first
                for q in range(6):
                    carry[2 + q] = carry[2 + q] + (is_second[q] * weight) * toward_second
            return tuple(carry)

        carry = (zero,) * 8
        steps = near_slots // unroll // group
        for g in range(group):
            if it == 0:
                near_load(g).wait()
            carry = lax.fori_loop(g * steps, (g + 1) * steps, near_slots_step, carry)
        for side, there in enumerate((me + n_clu - 1, me, me + 1)):
            base = pl.multiple_of(lax.rem(there, n_clu) * 2 * rows, 2 * rows)
            pair = jnp.concatenate([carry[2 + 2 * side], carry[3 + 2 * side]], axis=0)
            if side == 1:
                pair = pair + jnp.concatenate([carry[0], carry[1]], axis=0)
                pair = pair + first_far[: 2 * rows] + first_far[2 * rows :]
            sums[it, pl.ds(base, 2 * rows)] += pair
        sums_copy(it, 1).start()
        sums_copy(it, n_clu - 1).start()
        wait_all(sums_copy, it)
        total = sums[it, own_block]

        def add(d, total):
            return total + parts[it, lax.rem(me + d, n_clu)]

        total = lax.fori_loop(1, n_clu, add, total)
        return self_ref[...] * field + jnp.concatenate([total[:rows], total[rows:]], axis=1)

    wait_all(grid_copy, 0)
    loads[0].wait()
    loads[1].wait()
    image = apply(0, field)
    all_image[0, own] = image
    rhs_start(1, all_image.at[0])
    rhs_wait(1, all_image.at[0])
    slabs[1, me] = jnp.concatenate(
        [exact(image, all_image[0], NT), exact(image, all_right[...], NT)], axis=1
    )
    start_all(slab_copy, 1)
    wait_all(slab_copy, 0)
    wait_all(slab_copy, 1)
    grams[0, own] = jnp.concatenate([slab_sum(1), slab_sum(0)], axis=1)
    rhs_start(2, grams.at[0])
    rhs_wait(2, grams.at[0])

    count = n_rhs * rows
    together = grams[0]
    image_image = together[:, :count]
    image_right = together[:, count : 2 * count]
    norms = together[:, 128 : 128 + count]
    right_image = image_right.T
    curvature = 0.5 * (image_right + right_image)
    identity = jnp.where(
        lax.broadcasted_iota(jnp.int32, (count, count), 0)
        == lax.broadcasted_iota(jnp.int32, (count, count), 1),
        1.0,
        0.0,
    )
    alpha, inverse = solve_many(
        [
            jnp.concatenate([curvature, norms], axis=1),
            jnp.concatenate([norms, identity], axis=1),
        ]
    )
    crossed = exact(right_image, alpha, NN)
    next_norms = norms - crossed - crossed.T
    next_norms = next_norms + exact(alpha, exact(image_image, alpha, NN), TN)
    beta = exact(inverse, next_norms, NN)
    all_residual[...] = all_right[...] - exact(alpha, all_image[0], TN)
    all_direction[...] = all_residual[...] + exact(beta, all_right[...], TN)
    field = all_direction[own]
    set_charges(1, field)
    start_all(grid_copy, 1)
    slabs[2, me] = jnp.concatenate(
        [exact(all_residual[own], all_residual[...], NT), blank], axis=1
    )
    start_all(slab_copy, 2)
    first_solution[...] = exact(alpha, all_right[...], TN)
    wait_all(grid_copy, 1)
    image = apply(1, field)
    all_image[1, own] = image
    rhs_start(3, all_image.at[1])
    rhs_wait(3, all_image.at[1])
    slabs[3, me] = jnp.concatenate(
        [exact(all_direction[own], all_image[1], NT), blank], axis=1
    )
    start_all(slab_copy, 3)
    wait_all(slab_copy, 2)
    wait_all(slab_copy, 3)
    grams[1, own] = jnp.concatenate([slab_sum(3), slab_sum(2)], axis=1)
    rhs_start(4, grams.at[1])
    rhs_wait(4, grams.at[1])
    together = grams[1]
    curvature = together[:, :count]
    curvature = 0.5 * (curvature + curvature.T)
    (alpha,) = solve_many(
        [jnp.concatenate([curvature, together[:, 128 : 128 + count]], axis=1)]
    )
    first_solution[...] += exact(alpha, all_direction[...], TN)
    all_residual[...] = all_residual[...] - exact(alpha, all_image[1], TN)
    solution_ref[...] = first_solution[own]
    residual_ref[...] = all_residual[own]


def shards(
    mesh,
    right_side,
    self_term,
    near_pairs,
    near_blocks,
    near_scale,
    near_count,
    far_pairs,
    far_left,
    far_right,
    far_scale,
    far_rank,
    far_count,
):
    n_clu, n_rhs = mesh.shape["clu"], mesh.shape["rhs"]
    rows, width = right_side.shape
    near_slots = near_blocks.shape[0]
    far_slots, rank, _ = far_left.shape
    n_cl = 2 * n_clu
    count = rows * n_rhs
    far_rows = far_slots * rank
    vmem = pl.BlockSpec(memory_space=pltpu.VMEM)
    smem = pl.BlockSpec(memory_space=pltpu.SMEM)
    anywhere = pl.BlockSpec(memory_space=pl.ANY)
    field = jax.ShapeDtypeStruct((rows, width), F32)
    return pl.pallas_call(
        functools.partial(kernel, (n_clu, n_rhs, rows, near_slots, far_slots, rank)),
        out_shape=(field, field),
        in_specs=[vmem, vmem] + [smem] * 7 + [anywhere] * 3,
        out_specs=(vmem, vmem),
        scratch_shapes=[
            pltpu.VMEM(near_blocks.shape, BF16),
            pltpu.VMEM((far_rows, CLUSTER), BF16),
            pltpu.VMEM((far_rows, CLUSTER), BF16),
            pltpu.VMEM((1, far_rows), jnp.int32),
            pltpu.VMEM((1, far_rows), jnp.int32),
            pltpu.VMEM((1, far_rows), F32),
            pltpu.VMEM((1, far_rows), F32),
            pltpu.VMEM((n_cl * rows, far_rows), BF16),
            pltpu.VMEM((2, n_cl * rows, CLUSTER), BF16),
            pltpu.VMEM((6 * rows, CLUSTER), F32),
            pltpu.VMEM((2, n_cl * rows, CLUSTER), F32),
            pltpu.VMEM((2, n_clu, 2 * rows, CLUSTER), F32),
            pltpu.VMEM((4, n_clu, rows, 128), F32),
            pltpu.VMEM((count, width), F32),
            pltpu.VMEM((2, count, width), F32),
            pltpu.VMEM((count, width), F32),
            pltpu.VMEM((count, width), F32),
            pltpu.VMEM((2, count, 256), F32),
            pltpu.VMEM((count, width), F32),
            pltpu.SemaphoreType.DMA((6,)),
            pltpu.SemaphoreType.DMA((8, n_clu)),
            pltpu.SemaphoreType.DMA((8, n_clu)),
            pltpu.SemaphoreType.DMA((5, n_rhs)),
            pltpu.SemaphoreType.DMA((5, n_rhs)),
        ],
        compiler_params=pltpu.CompilerParams(
            collective_id=0, has_side_effects=True, vmem_limit_bytes=48 * 1024 * 1024
        ),
        name="block_cg",
    )(
        right_side,
        self_term.reshape(1, width),
        near_pairs,
        near_scale,
        near_count,
        far_pairs,
        far_scale,
        far_rank,
        far_count,
        near_blocks,
        far_left.reshape(far_rows, CLUSTER),
        far_right.reshape(far_rows, CLUSTER),
    )


def solution(mesh):
    placed = (
        P("rhs", "clu"),
        P("clu"),
        P("clu", None),
        P("clu", None, None),
        P("clu"),
        P("clu"),
        P("clu", None),
        P("clu", None, None),
        P("clu", None, None),
        P("clu"),
        P("clu"),
        P("clu"),
    )
    return jax.shard_map(
        functools.partial(shards, mesh),
        mesh=mesh,
        in_specs=placed,
        out_specs=(P("rhs", "clu"), P("rhs", "clu")),
        check_vma=False,
    )
```

```python
import functools

import jax
import jax.numpy as jnp
from jax import lax
from jax.experimental import pallas as pl
from jax.experimental.pallas import tpu as pltpu
from jax.sharding import PartitionSpec as P

CLUSTER = 256
PRECISE = lax.Precision.HIGHEST
F32 = jnp.float32
BF16 = jnp.bfloat16
MESH = pl.DeviceIdType.MESH

NT = (((1,), (1,)), ((), ()))
NN = (((1,), (0,)), ((), ()))
TN = (((0,), (0,)), ((), ()))


def dot(left, right, dims):
    return lax.dot_general(left, right, dims, preferred_element_type=F32)


def exact(left, right, dims):
    return lax.dot_general(left, right, dims, precision=PRECISE, preferred_element_type=F32)


def solve_many(systems):
    size, wide = systems[0].shape
    step = 8
    row_at = lax.broadcasted_iota(jnp.int32, (size, 1), 0)

    def block(_, current):
        current = list(current)
        for k in range(0, step, 2):
            for at, m in enumerate(current):
                left = jnp.broadcast_to(m[:, k : k + 1], m.shape)
                right = jnp.broadcast_to(m[:, k + 1 : k + 2], m.shape)
                upper, lower = m[k : k + 1, :], m[k + 1 : k + 2, :]
                turn = 1.0 / left[k : k + 1, :]
                ratio = left[k + 1 : k + 2, :] * turn
                corner = right[k : k + 1, :]
                second = (lower - ratio * upper) * (
                    1.0 / (right[k + 1 : k + 2, :] - ratio * corner)
                )
                first = (upper - corner * second) * turn
                rest = m - left * first - right * second
                rest = jnp.where(row_at == k, first, rest)
                current[at] = jnp.where(row_at == k + 1, second, rest)
        return tuple(
            pltpu.roll(jnp.concatenate([m[step:], m[:step]], axis=0), wide - step, 1)
            for m in current
        )

    done = lax.fori_loop(0, size // step, block, tuple(systems))
    return [m[:, : wide - size] for m in done]


def kernel(
    sizes,
    right_hbm,
    self_hbm,
    near_pairs_hbm,
    near_scale_hbm,
    near_count_hbm,
    far_pairs_hbm,
    far_scale_hbm,
    far_rank_hbm,
    far_count_hbm,
    near_hbm,
    left_hbm,
    rightf_hbm,
    solution_ref,
    residual_ref,
    right_ref,
    self_ref,
    near_pairs,
    near_scale,
    near_count,
    far_pairs,
    far_scale,
    far_rank,
    far_count,
    near,
    far_l,
    far_r,
    meta_i,
    meta_j,
    meta_keep,
    meta_w,
    lhs,
    grid,
    around,
    sums,
    parts,
    slabs,
    all_right,
    all_image,
    all_direction,
    all_residual,
    grams,
    first_solution,
    small_sem,
    load_sem,
    clu_send,
    clu_recv,
    rhs_send,
    rhs_recv,
):
    n_clu, n_rhs, rows, near_slots, far_slots, rank = sizes
    me, col = lax.axis_index("clu"), lax.axis_index("rhs")
    n_cl = 2 * n_clu
    own = pl.ds(pl.multiple_of(col * rows, rows), rows)
    own_block = pl.ds(pl.multiple_of(me * 2 * rows, 2 * rows), 2 * rows)
    tile = 256
    slots_tile = tile // rank
    tiles = far_slots // slots_tile
    group = 4

    small = [
        pltpu.make_async_copy(src, dst, small_sem.at[k])
        for k, (src, dst) in enumerate(
            (
                (right_hbm, right_ref),
                (self_hbm, self_ref),
                (near_pairs_hbm, near_pairs),
                (near_scale_hbm, near_scale),
                (near_count_hbm, near_count),
                (far_pairs_hbm, far_pairs),
                (far_scale_hbm, far_scale),
                (far_rank_hbm, far_rank),
                (far_count_hbm, far_count),
            )
        )
    ]
    for load in small:
        load.start()

    def near_load(g):
        part = pl.ds(g * (near_slots // group), near_slots // group)
        return pltpu.make_async_copy(near_hbm.at[part], near.at[part], load_sem.at[2 + g])

    loads = [
        pltpu.make_async_copy(left_hbm, far_l, load_sem.at[0]),
        pltpu.make_async_copy(rightf_hbm, far_r, load_sem.at[1]),
    ] + [near_load(g) for g in range(group)]
    for load in loads:
        load.start()

    barrier = pltpu.get_barrier_semaphore()

    @pl.loop(1, n_clu)
    def _(d):
        pl.semaphore_signal(
            barrier, inc=1, device_id={"clu": lax.rem(me + d, n_clu)}, device_id_type=MESH
        )

    for d in range(1, n_rhs):
        pl.semaphore_signal(
            barrier, inc=1, device_id={"rhs": lax.rem(col + d, n_rhs)}, device_id_type=MESH
        )

    def clu_copy(kind, d, src, dst):
        return pltpu.make_async_remote_copy(
            src_ref=src,
            dst_ref=dst,
            send_sem=clu_send.at[kind, d],
            recv_sem=clu_recv.at[kind, d],
            device_id={"clu": lax.rem(me + d, n_clu)},
            device_id_type=MESH,
        )

    def rhs_copy(kind, d, ref):
        return pltpu.make_async_remote_copy(
            src_ref=ref.at[own],
            dst_ref=ref.at[own],
            send_sem=rhs_send.at[kind, d],
            recv_sem=rhs_recv.at[kind, d],
            device_id={"rhs": lax.rem(col + d, n_rhs)},
            device_id_type=MESH,
        )

    def rhs_start(kind, ref):
        for d in range(1, n_rhs):
            rhs_copy(kind, d, ref).start()

    def rhs_wait(kind, ref):
        for d in range(1, n_rhs):
            rhs_copy(kind, d, ref).wait()

    def grid_copy(it, d):
        block = grid.at[it, own_block]
        return clu_copy(it, d, block, block)

    def slab_copy(which, d):
        block = slabs.at[which, me]
        return clu_copy(4 + which, d, block, block)

    def sums_copy(it, d):
        there = lax.rem(me + d, n_clu)
        src = sums.at[it, pl.ds(pl.multiple_of(there * 2 * rows, 2 * rows), 2 * rows)]
        return clu_copy(2 + it, d, src, parts.at[it, me])

    def start_all(copy, which):
        @pl.loop(1, n_clu)
        def _(d):
            copy(which, d).start()

    def wait_all(copy, which):
        @pl.loop(1, n_clu)
        def _(d):
            copy(which, d).wait()

    def set_charges(it, field):
        grid[it, own_block] = jnp.concatenate(
            [field[:, :CLUSTER], field[:, CLUSTER:]], axis=0
        ).astype(BF16)

    def slab_sum(which):
        return lax.fori_loop(
            1, n_clu, lambda k, total: total + slabs[which, k], slabs[which, 0]
        )

    small[0].wait()
    field = right_ref[...]
    set_charges(0, field)
    all_right[own] = field
    pl.semaphore_wait(barrier, n_clu + n_rhs - 2)
    start_all(grid_copy, 0)
    rhs_start(0, all_right)

    for load in small[1:]:
        load.wait()

    lane = lax.broadcasted_iota(jnp.int32, (1, 128), 1)
    slot_in = lane // rank
    live = far_count[0]
    per = 128 // rank
    for g in range(far_slots // per):
        at = slice(g * 128, (g + 1) * 128)

        def spread(value):
            out = jnp.full((1, 128), value(g * per))
            for q in range(1, per):
                out = jnp.where(slot_in == q, value(g * per + q), out)
            return out

        meta_i[:, at] = spread(lambda s: far_pairs[0, s])
        meta_j[:, at] = spread(lambda s: far_pairs[1, s])
        meta_keep[:, at] = jnp.where(
            lane - slot_in * rank < spread(lambda s: far_rank[s]), 1.0, 0.0
        )
        meta_w[:, at] = spread(
            lambda s: jnp.where(s < live, far_scale[s], jnp.zeros((), F32))
        )

    rhs_wait(0, all_right)
    blank = jnp.zeros((rows, 128 - n_rhs * rows), F32)
    slabs[0, me] = jnp.concatenate([exact(all_right[own], all_right[...], NT), blank], axis=1)
    start_all(slab_copy, 0)

    def apply(it, field):
        first_far = jnp.zeros((4 * rows, CLUSTER), F32)
        for t in range(tiles):
            at = slice(t * tile, (t + 1) * tile)
            right_tile, left_tile = far_r[at, :], far_l[at, :]
            to_i, to_j = meta_i[:, at], meta_j[:, at]
            keep, weight = meta_keep[:, at], meta_w[:, at]

            def pick(b, coef):
                base = pl.multiple_of(b * 16 * rows, 16 * rows)
                product = dot(grid[it, pl.ds(base, 16 * rows)], right_tile, NT)
                for q in range(16):
                    coef = coef + jnp.where(
                        to_j == b * 16 + q, product[q * rows : (q + 1) * rows], 0.0
                    )
                return coef

            coef_second = jnp.zeros((rows, tile), F32)
            if n_cl == 16:
                coef_second = pick(0, coef_second)
            else:
                coef_second = lax.fori_loop(0, n_cl // 16, pick, coef_second)
            coef_second = jnp.where(keep > 0.0, coef_second, 0.0).astype(BF16).astype(F32) * weight
            high = coef_second.astype(BF16).astype(F32)
            low = coef_second - high
            low_cluster = to_i == 2 * me
            stack = jnp.concatenate(
                [
                    jnp.where(low_cluster, high, 0.0),
                    jnp.where(low_cluster, 0.0, high),
                    jnp.where(low_cluster, low, 0.0),
                    jnp.where(low_cluster, 0.0, low),
                ],
                axis=0,
            ).astype(BF16)
            first_far = first_far + dot(stack, left_tile, NN)
            both = dot(grid[it, own_block], left_tile, NT)
            coef_first = jnp.where(low_cluster, both[:rows], both[rows:]) * weight
            coef_first = jnp.where(keep > 0.0, coef_first, 0.0)

            def spread_rows(b, carry):
                for q in range(16):
                    base = pl.multiple_of(b * 16 * rows + q * rows, rows)
                    lhs[pl.ds(base, rows), at] = jnp.where(
                        to_j == b * 16 + q, coef_first, 0.0
                    ).astype(BF16)
                return carry

            if n_cl == 16:
                spread_rows(0, 0)
            else:
                lax.fori_loop(0, n_cl // 16, spread_rows, 0)

        def second_far(b, carry):
            part = pl.ds(pl.multiple_of(b * 16 * rows, 16 * rows), 16 * rows)
            sums[it, part] = dot(lhs[part], far_r[...], NN)
            return carry

        lax.fori_loop(0, n_cl // 16, second_far, 0)

        @pl.loop(2, n_clu - 1)
        def _(d):
            sums_copy(it, d).start()

        for side, there in enumerate((me + n_clu - 1, me, me + 1)):
            base = pl.multiple_of(lax.rem(there, n_clu) * 2 * rows, 2 * rows)
            around[side * 2 * rows : (side + 1) * 2 * rows] = grid[
                it, pl.ds(base, 2 * rows)
            ].astype(F32)
        near_live = near_count[0]
        unroll = 4
        zero = jnp.zeros((rows, CLUSTER), F32)

        def near_slots_step(g, carry):
            carry = list(carry)
            for u in range(unroll):
                s = g * unroll + u
                i, j = near_pairs[0, s], near_pairs[1, s]
                weight = jnp.where(s < near_live, near_scale[s], jnp.zeros((), F32))
                block = near[s]
                offset = j - 2 * me + 2
                offset = jnp.where(offset < 0, offset + n_cl, offset)
                offset = jnp.where(offset >= n_cl, offset - n_cl, offset)
                is_first = [jnp.where(i - 2 * me == q, 1.0, 0.0) for q in range(2)]
                is_second = [jnp.where(offset == q, 1.0, 0.0) for q in range(6)]
                first = is_first[0] * around[2 * rows : 3 * rows]
                first = first + is_first[1] * around[3 * rows : 4 * rows]
                second = is_second[0] * around[:rows]
                for q in range(1, 6):
                    second = second + is_second[q] * around[q * rows : (q + 1) * rows]
                toward_first = dot(second.astype(BF16), block, NT)
                toward_second = dot(first.astype(BF16), block, NN)
                for q in range(2):
                    carry[q] = carry[q] + (is_first[q] * weight) * toward_first
                for q in range(6):
                    carry[2 + q] = carry[2 + q] + (is_second[q] * weight) * toward_second
            return tuple(carry)

        carry = (zero,) * 8
        steps = near_slots // unroll // group
        for g in range(group):
            if it == 0:
                near_load(g).wait()
            carry = lax.fori_loop(g * steps, (g + 1) * steps, near_slots_step, carry)
        for side, there in enumerate((me + n_clu - 1, me, me + 1)):
            base = pl.multiple_of(lax.rem(there, n_clu) * 2 * rows, 2 * rows)
            pair = jnp.concatenate([carry[2 + 2 * side], carry[3 + 2 * side]], axis=0)
            if side == 1:
                pair = pair + jnp.concatenate([carry[0], carry[1]], axis=0)
                pair = pair + first_far[: 2 * rows] + first_far[2 * rows :]
            sums[it, pl.ds(base, 2 * rows)] += pair
        sums_copy(it, 1).start()
        sums_copy(it, n_clu - 1).start()
        wait_all(sums_copy, it)
        total = sums[it, own_block]

        def add(d, total):
            return total + parts[it, lax.rem(me + d, n_clu)]

        total = lax.fori_loop(1, n_clu, add, total)
        return self_ref[...] * field + jnp.concatenate([total[:rows], total[rows:]], axis=1)

    wait_all(grid_copy, 0)
    loads[0].wait()
    loads[1].wait()
    image = apply(0, field)
    all_image[0, own] = image
    rhs_start(1, all_image.at[0])
    rhs_wait(1, all_image.at[0])
    slabs[1, me] = jnp.concatenate(
        [exact(image, all_image[0], NT), exact(image, all_right[...], NT)], axis=1
    )
    start_all(slab_copy, 1)
    wait_all(slab_copy, 0)
    wait_all(slab_copy, 1)
    grams[0, own] = jnp.concatenate([slab_sum(1), slab_sum(0)], axis=1)
    rhs_start(2, grams.at[0])
    rhs_wait(2, grams.at[0])

    count = n_rhs * rows
    together = grams[0]
    image_image = together[:, :count]
    image_right = together[:, count : 2 * count]
    norms = together[:, 128 : 128 + count]
    right_image = image_right.T
    curvature = 0.5 * (image_right + right_image)
    identity = jnp.where(
        lax.broadcasted_iota(jnp.int32, (count, count), 0)
        == lax.broadcasted_iota(jnp.int32, (count, count), 1),
        1.0,
        0.0,
    )
    alpha, inverse = solve_many(
        [
            jnp.concatenate([curvature, norms], axis=1),
            jnp.concatenate([norms, identity], axis=1),
        ]
    )
    crossed = exact(right_image, alpha, NN)
    next_norms = norms - crossed - crossed.T
    next_norms = next_norms + exact(alpha, exact(image_image, alpha, NN), TN)
    beta = exact(inverse, next_norms, NN)
    all_residual[...] = all_right[...] - exact(alpha, all_image[0], TN)
    all_direction[...] = all_residual[...] + exact(beta, all_right[...], TN)
    field = all_direction[own]
    set_charges(1, field)
    start_all(grid_copy, 1)
    slabs[2, me] = jnp.concatenate(
        [exact(all_residual[own], all_residual[...], NT), blank], axis=1
    )
    start_all(slab_copy, 2)
    first_solution[...] = exact(alpha, all_right[...], TN)
    wait_all(grid_copy, 1)
    image = apply(1, field)
    all_image[1, own] = image
    rhs_start(3, all_image.at[1])
    rhs_wait(3, all_image.at[1])
    slabs[3, me] = jnp.concatenate(
        [exact(all_direction[own], all_image[1], NT), blank], axis=1
    )
    start_all(slab_copy, 3)
    wait_all(slab_copy, 2)
    wait_all(slab_copy, 3)
    grams[1, own] = jnp.concatenate([slab_sum(3), slab_sum(2)], axis=1)
    rhs_start(4, grams.at[1])
    rhs_wait(4, grams.at[1])
    together = grams[1]
    curvature = together[:, :count]
    curvature = 0.5 * (curvature + curvature.T)
    (alpha,) = solve_many(
        [jnp.concatenate([curvature, together[:, 128 : 128 + count]], axis=1)]
    )
    first_solution[...] += exact(alpha, all_direction[...], TN)
    all_residual[...] = all_residual[...] - exact(alpha, all_image[1], TN)
    solution_ref[...] = first_solution[own]
    residual_ref[...] = all_residual[own]


def shards(
    mesh,
    right_side,
    self_term,
    near_pairs,
    near_blocks,
    near_scale,
    near_count,
    far_pairs,
    far_left,
    far_right,
    far_scale,
    far_rank,
    far_count,
):
    n_clu, n_rhs = mesh.shape["clu"], mesh.shape["rhs"]
    rows, width = right_side.shape
    near_slots = near_blocks.shape[0]
    far_slots, rank, _ = far_left.shape
    n_cl = 2 * n_clu
    count = rows * n_rhs
    far_rows = far_slots * rank
    vmem = pl.BlockSpec(memory_space=pltpu.VMEM)
    hbm = pl.BlockSpec(memory_space=pltpu.HBM)
    field = jax.ShapeDtypeStruct((rows, width), F32)
    return pl.pallas_call(
        functools.partial(kernel, (n_clu, n_rhs, rows, near_slots, far_slots, rank)),
        out_shape=(field, field),
        in_specs=[hbm] * 12,
        out_specs=(vmem, vmem),
        scratch_shapes=[
            pltpu.VMEM((rows, width), F32),
            pltpu.VMEM((1, width), F32),
            pltpu.SMEM((2, near_slots), jnp.int32),
            pltpu.SMEM((near_slots,), F32),
            pltpu.SMEM((1,), jnp.int32),
            pltpu.SMEM((2, far_slots), jnp.int32),
            pltpu.SMEM((far_slots,), F32),
            pltpu.SMEM((far_slots,), jnp.int32),
            pltpu.SMEM((1,), jnp.int32),
            pltpu.VMEM(near_blocks.shape, BF16),
            pltpu.VMEM((far_rows, CLUSTER), BF16),
            pltpu.VMEM((far_rows, CLUSTER), BF16),
            pltpu.VMEM((1, far_rows), jnp.int32),
            pltpu.VMEM((1, far_rows), jnp.int32),
            pltpu.VMEM((1, far_rows), F32),
            pltpu.VMEM((1, far_rows), F32),
            pltpu.VMEM((n_cl * rows, far_rows), BF16),
            pltpu.VMEM((2, n_cl * rows, CLUSTER), BF16),
            pltpu.VMEM((6 * rows, CLUSTER), F32),
            pltpu.VMEM((2, n_cl * rows, CLUSTER), F32),
            pltpu.VMEM((2, n_clu, 2 * rows, CLUSTER), F32),
            pltpu.VMEM((4, n_clu, rows, 128), F32),
            pltpu.VMEM((count, width), F32),
            pltpu.VMEM((2, count, width), F32),
            pltpu.VMEM((count, width), F32),
            pltpu.VMEM((count, width), F32),
            pltpu.VMEM((2, count, 256), F32),
            pltpu.VMEM((count, width), F32),
            pltpu.SemaphoreType.DMA((9,)),
            pltpu.SemaphoreType.DMA((6,)),
            pltpu.SemaphoreType.DMA((8, n_clu)),
            pltpu.SemaphoreType.DMA((8, n_clu)),
            pltpu.SemaphoreType.DMA((5, n_rhs)),
            pltpu.SemaphoreType.DMA((5, n_rhs)),
        ],
        compiler_params=pltpu.CompilerParams(
            collective_id=0, has_side_effects=True, vmem_limit_bytes=64 * 1024 * 1024
        ),
        name="block_cg",
    )(
        right_side,
        self_term.reshape(1, width),
        near_pairs.T,
        near_scale,
        near_count,
        far_pairs.T,
        far_scale,
        far_rank,
        far_count,
        near_blocks,
        far_left.reshape(far_rows, CLUSTER),
        far_right.reshape(far_rows, CLUSTER),
    )


def solution(mesh):
    placed = (
        P("rhs", "clu"),
        P("clu"),
        P("clu", None),
        P("clu", None, None),
        P("clu"),
        P("clu"),
        P("clu", None),
        P("clu", None, None),
        P("clu", None, None),
        P("clu"),
        P("clu"),
        P("clu"),
    )
    return jax.shard_map(
        functools.partial(shards, mesh),
        mesh=mesh,
        in_specs=placed,
        out_specs=(P("rhs", "clu"), P("rhs", "clu")),
        check_vma=False,
    )
```

```python
import functools

import jax
import jax.numpy as jnp
from jax import lax
from jax.experimental import pallas as pl
from jax.experimental.pallas import tpu as pltpu
from jax.sharding import PartitionSpec as P

CLUSTER = 256
PRECISE = lax.Precision.HIGHEST
F32 = jnp.float32
BF16 = jnp.bfloat16
MESH = pl.DeviceIdType.MESH

NT = (((1,), (1,)), ((), ()))
NN = (((1,), (0,)), ((), ()))
TN = (((0,), (0,)), ((), ()))


def dot(left, right, dims):
    return lax.dot_general(left, right, dims, preferred_element_type=F32)


def exact(left, right, dims):
    return lax.dot_general(left, right, dims, precision=PRECISE, preferred_element_type=F32)


def solve_many(systems):
    size, wide = systems[0].shape
    step = 32
    row_at = lax.broadcasted_iota(jnp.int32, (size, 1), 0)

    def block(_, current):
        current = list(current)
        for k in range(0, step, 2):
            for at, m in enumerate(current):
                left = jnp.broadcast_to(m[:, k : k + 1], m.shape)
                right = jnp.broadcast_to(m[:, k + 1 : k + 2], m.shape)
                upper, lower = m[k : k + 1, :], m[k + 1 : k + 2, :]
                turn = 1.0 / left[k : k + 1, :]
                ratio = left[k + 1 : k + 2, :] * turn
                corner = right[k : k + 1, :]
                second = (lower - ratio * upper) * (
                    1.0 / (right[k + 1 : k + 2, :] - ratio * corner)
                )
                first = (upper - corner * second) * turn
                rest = m - left * first - right * second
                rest = jnp.where(row_at == k, first, rest)
                current[at] = jnp.where(row_at == k + 1, second, rest)
        return tuple(
            pltpu.roll(jnp.concatenate([m[step:], m[:step]], axis=0), wide - step, 1)
            for m in current
        )

    done = lax.fori_loop(0, size // step, block, tuple(systems))
    return [m[:, : wide - size] for m in done]


def kernel(
    sizes,
    right_hbm,
    self_hbm,
    near_pairs_hbm,
    near_scale_hbm,
    near_count_hbm,
    far_pairs_hbm,
    far_scale_hbm,
    far_rank_hbm,
    far_count_hbm,
    near_hbm,
    left_hbm,
    rightf_hbm,
    solution_ref,
    residual_ref,
    right_ref,
    self_ref,
    near_pairs,
    near_scale,
    near_count,
    far_pairs,
    far_scale,
    far_rank,
    far_count,
    near,
    far_l,
    far_r,
    meta_i,
    meta_j,
    meta_keep,
    meta_w,
    lhs,
    grid,
    around,
    sums,
    parts,
    slabs,
    all_right,
    all_image,
    all_direction,
    all_residual,
    grams,
    first_solution,
    small_sem,
    load_sem,
    clu_send,
    clu_recv,
    rhs_send,
    rhs_recv,
):
    n_clu, n_rhs, rows, near_slots, far_slots, rank = sizes
    me, col = lax.axis_index("clu"), lax.axis_index("rhs")
    n_cl = 2 * n_clu
    own = pl.ds(pl.multiple_of(col * rows, rows), rows)
    own_block = pl.ds(pl.multiple_of(me * 2 * rows, 2 * rows), 2 * rows)
    tile = 256
    slots_tile = tile // rank
    tiles = far_slots // slots_tile
    group = 4

    small = [
        pltpu.make_async_copy(src, dst, small_sem.at[k])
        for k, (src, dst) in enumerate(
            (
                (right_hbm, right_ref),
                (self_hbm, self_ref),
                (near_pairs_hbm, near_pairs),
                (near_scale_hbm, near_scale),
                (near_count_hbm, near_count),
                (far_pairs_hbm, far_pairs),
                (far_scale_hbm, far_scale),
                (far_rank_hbm, far_rank),
                (far_count_hbm, far_count),
            )
        )
    ]
    for load in small:
        load.start()

    def near_load(g):
        part = pl.ds(g * (near_slots // group), near_slots // group)
        return pltpu.make_async_copy(near_hbm.at[part], near.at[part], load_sem.at[2 + g])

    loads = [
        pltpu.make_async_copy(left_hbm, far_l, load_sem.at[0]),
        pltpu.make_async_copy(rightf_hbm, far_r, load_sem.at[1]),
    ] + [near_load(g) for g in range(group)]
    for load in loads:
        load.start()

    barrier = pltpu.get_barrier_semaphore()

    @pl.loop(1, n_clu)
    def _(d):
        pl.semaphore_signal(
            barrier, inc=1, device_id={"clu": lax.rem(me + d, n_clu)}, device_id_type=MESH
        )

    for d in range(1, n_rhs):
        pl.semaphore_signal(
            barrier, inc=1, device_id={"rhs": lax.rem(col + d, n_rhs)}, device_id_type=MESH
        )

    def clu_copy(kind, d, src, dst):
        return pltpu.make_async_remote_copy(
            src_ref=src,
            dst_ref=dst,
            send_sem=clu_send.at[kind, d],
            recv_sem=clu_recv.at[kind, d],
            device_id={"clu": lax.rem(me + d, n_clu)},
            device_id_type=MESH,
        )

    def rhs_copy(kind, d, ref):
        return pltpu.make_async_remote_copy(
            src_ref=ref.at[own],
            dst_ref=ref.at[own],
            send_sem=rhs_send.at[kind, d],
            recv_sem=rhs_recv.at[kind, d],
            device_id={"rhs": lax.rem(col + d, n_rhs)},
            device_id_type=MESH,
        )

    def rhs_start(kind, ref):
        for d in range(1, n_rhs):
            rhs_copy(kind, d, ref).start()

    def rhs_wait(kind, ref):
        for d in range(1, n_rhs):
            rhs_copy(kind, d, ref).wait()

    def grid_copy(it, d):
        block = grid.at[it, own_block]
        return clu_copy(it, d, block, block)

    def slab_copy(which, d):
        block = slabs.at[which, me]
        return clu_copy(4 + which, d, block, block)

    def sums_copy(it, d):
        there = lax.rem(me + d, n_clu)
        src = sums.at[it, pl.ds(pl.multiple_of(there * 2 * rows, 2 * rows), 2 * rows)]
        return clu_copy(2 + it, d, src, parts.at[it, me])

    def start_all(copy, which):
        @pl.loop(1, n_clu)
        def _(d):
            copy(which, d).start()

    def wait_all(copy, which):
        @pl.loop(1, n_clu)
        def _(d):
            copy(which, d).wait()

    def set_charges(it, field):
        grid[it, own_block] = jnp.concatenate(
            [field[:, :CLUSTER], field[:, CLUSTER:]], axis=0
        ).astype(BF16)

    def slab_sum(which):
        return lax.fori_loop(
            1, n_clu, lambda k, total: total + slabs[which, k], slabs[which, 0]
        )

    small[0].wait()
    field = right_ref[...]
    set_charges(0, field)
    all_right[own] = field
    pl.semaphore_wait(barrier, n_clu + n_rhs - 2)
    start_all(grid_copy, 0)
    rhs_start(0, all_right)

    for load in small[1:]:
        load.wait()

    lane = lax.broadcasted_iota(jnp.int32, (1, 128), 1)
    slot_in = lane // rank
    live = far_count[0]
    per = 128 // rank
    for g in range(far_slots // per):
        at = slice(g * 128, (g + 1) * 128)

        def spread(value):
            out = jnp.full((1, 128), value(g * per))
            for q in range(1, per):
                out = jnp.where(slot_in == q, value(g * per + q), out)
            return out

        meta_i[:, at] = spread(lambda s: far_pairs[0, s])
        meta_j[:, at] = spread(lambda s: far_pairs[1, s])
        meta_keep[:, at] = jnp.where(
            lane - slot_in * rank < spread(lambda s: far_rank[s]), 1.0, 0.0
        )
        meta_w[:, at] = spread(
            lambda s: jnp.where(s < live, far_scale[s], jnp.zeros((), F32))
        )

    rhs_wait(0, all_right)
    blank = jnp.zeros((rows, 128 - n_rhs * rows), F32)
    slabs[0, me] = jnp.concatenate([exact(all_right[own], all_right[...], NT), blank], axis=1)
    start_all(slab_copy, 0)

    def apply(it, field):
        first_far = jnp.zeros((4 * rows, CLUSTER), F32)
        for t in range(tiles):
            at = slice(t * tile, (t + 1) * tile)
            right_tile, left_tile = far_r[at, :], far_l[at, :]
            to_i, to_j = meta_i[:, at], meta_j[:, at]
            keep, weight = meta_keep[:, at], meta_w[:, at]

            def pick(b, coef):
                base = pl.multiple_of(b * 16 * rows, 16 * rows)
                product = dot(grid[it, pl.ds(base, 16 * rows)], right_tile, NT)
                for q in range(16):
                    coef = coef + jnp.where(
                        to_j == b * 16 + q, product[q * rows : (q + 1) * rows], 0.0
                    )
                return coef

            coef_second = jnp.zeros((rows, tile), F32)
            if n_cl == 16:
                coef_second = pick(0, coef_second)
            else:
                coef_second = lax.fori_loop(0, n_cl // 16, pick, coef_second)
            coef_second = jnp.where(keep > 0.0, coef_second, 0.0).astype(BF16).astype(F32) * weight
            high = coef_second.astype(BF16).astype(F32)
            low = coef_second - high
            low_cluster = to_i == 2 * me
            stack = jnp.concatenate(
                [
                    jnp.where(low_cluster, high, 0.0),
                    jnp.where(low_cluster, 0.0, high),
                    jnp.where(low_cluster, low, 0.0),
                    jnp.where(low_cluster, 0.0, low),
                ],
                axis=0,
            ).astype(BF16)
            first_far = first_far + dot(stack, left_tile, NN)
            both = dot(grid[it, own_block], left_tile, NT)
            coef_first = jnp.where(low_cluster, both[:rows], both[rows:]) * weight
            coef_first = jnp.where(keep > 0.0, coef_first, 0.0)

            def spread_rows(b, carry):
                for q in range(16):
                    base = pl.multiple_of(b * 16 * rows + q * rows, rows)
                    lhs[pl.ds(base, rows), at] = jnp.where(
                        to_j == b * 16 + q, coef_first, 0.0
                    ).astype(BF16)
                return carry

            if n_cl == 16:
                spread_rows(0, 0)
            else:
                lax.fori_loop(0, n_cl // 16, spread_rows, 0)

        def second_far(b, carry):
            part = pl.ds(pl.multiple_of(b * 16 * rows, 16 * rows), 16 * rows)
            sums[it, part] = dot(lhs[part], far_r[...], NN)
            return carry

        lax.fori_loop(0, n_cl // 16, second_far, 0)

        @pl.loop(2, n_clu - 1)
        def _(d):
            sums_copy(it, d).start()

        for side, there in enumerate((me + n_clu - 1, me, me + 1)):
            base = pl.multiple_of(lax.rem(there, n_clu) * 2 * rows, 2 * rows)
            around[side * 2 * rows : (side + 1) * 2 * rows] = grid[
                it, pl.ds(base, 2 * rows)
            ].astype(F32)
        near_live = near_count[0]
        unroll = 16
        zero = jnp.zeros((rows, CLUSTER), F32)

        def near_slots_step(g, carry):
            carry = list(carry)
            for u in range(unroll):
                s = g * unroll + u
                i, j = near_pairs[0, s], near_pairs[1, s]
                weight = jnp.where(s < near_live, near_scale[s], jnp.zeros((), F32))
                block = near[s]
                offset = j - 2 * me + 2
                offset = jnp.where(offset < 0, offset + n_cl, offset)
                offset = jnp.where(offset >= n_cl, offset - n_cl, offset)
                is_first = [jnp.where(i - 2 * me == q, 1.0, 0.0) for q in range(2)]
                is_second = [jnp.where(offset == q, 1.0, 0.0) for q in range(6)]
                first = is_first[0] * around[2 * rows : 3 * rows]
                first = first + is_first[1] * around[3 * rows : 4 * rows]
                second = is_second[0] * around[:rows]
                for q in range(1, 6):
                    second = second + is_second[q] * around[q * rows : (q + 1) * rows]
                toward_first = dot(second.astype(BF16), block, NT)
                toward_second = dot(first.astype(BF16), block, NN)
                for q in range(2):
                    carry[q] = carry[q] + (is_first[q] * weight) * toward_first
                for q in range(6):
                    carry[2 + q] = carry[2 + q] + (is_second[q] * weight) * toward_second
            return tuple(carry)

        carry = (zero,) * 8
        steps = near_slots // unroll // group
        for g in range(group):
            if it == 0:
                near_load(g).wait()
            carry = lax.fori_loop(g * steps, (g + 1) * steps, near_slots_step, carry)
        for side, there in enumerate((me + n_clu - 1, me, me + 1)):
            base = pl.multiple_of(lax.rem(there, n_clu) * 2 * rows, 2 * rows)
            pair = jnp.concatenate([carry[2 + 2 * side], carry[3 + 2 * side]], axis=0)
            if side == 1:
                pair = pair + jnp.concatenate([carry[0], carry[1]], axis=0)
                pair = pair + first_far[: 2 * rows] + first_far[2 * rows :]
            sums[it, pl.ds(base, 2 * rows)] += pair
        sums_copy(it, 1).start()
        sums_copy(it, n_clu - 1).start()
        wait_all(sums_copy, it)
        total = sums[it, own_block]

        def add(d, total):
            return total + parts[it, lax.rem(me + d, n_clu)]

        total = lax.fori_loop(1, n_clu, add, total)
        return self_ref[...] * field + jnp.concatenate([total[:rows], total[rows:]], axis=1)

    wait_all(grid_copy, 0)
    loads[0].wait()
    loads[1].wait()
    image = apply(0, field)
    all_image[0, own] = image
    rhs_start(1, all_image.at[0])
    rhs_wait(1, all_image.at[0])
    slabs[1, me] = jnp.concatenate(
        [exact(image, all_image[0], NT), exact(image, all_right[...], NT)], axis=1
    )
    start_all(slab_copy, 1)
    wait_all(slab_copy, 0)
    wait_all(slab_copy, 1)
    grams[0, own] = jnp.concatenate([slab_sum(1), slab_sum(0)], axis=1)
    rhs_start(2, grams.at[0])
    rhs_wait(2, grams.at[0])

    count = n_rhs * rows
    together = grams[0]
    image_image = together[:, :count]
    image_right = together[:, count : 2 * count]
    norms = together[:, 128 : 128 + count]
    right_image = image_right.T
    curvature = 0.5 * (image_right + right_image)
    identity = jnp.where(
        lax.broadcasted_iota(jnp.int32, (count, count), 0)
        == lax.broadcasted_iota(jnp.int32, (count, count), 1),
        1.0,
        0.0,
    )
    alpha, inverse = solve_many(
        [
            jnp.concatenate([curvature, norms], axis=1),
            jnp.concatenate([norms, identity], axis=1),
        ]
    )
    crossed = exact(right_image, alpha, NN)
    next_norms = norms - crossed - crossed.T
    next_norms = next_norms + exact(alpha, exact(image_image, alpha, NN), TN)
    beta = exact(inverse, next_norms, NN)
    all_residual[...] = all_right[...] - exact(alpha, all_image[0], TN)
    all_direction[...] = all_residual[...] + exact(beta, all_right[...], TN)
    field = all_direction[own]
    set_charges(1, field)
    start_all(grid_copy, 1)
    slabs[2, me] = jnp.concatenate(
        [exact(all_residual[own], all_residual[...], NT), blank], axis=1
    )
    start_all(slab_copy, 2)
    first_solution[...] = exact(alpha, all_right[...], TN)
    wait_all(grid_copy, 1)
    image = apply(1, field)
    all_image[1, own] = image
    rhs_start(3, all_image.at[1])
    rhs_wait(3, all_image.at[1])
    slabs[3, me] = jnp.concatenate(
        [exact(all_direction[own], all_image[1], NT), blank], axis=1
    )
    start_all(slab_copy, 3)
    wait_all(slab_copy, 2)
    wait_all(slab_copy, 3)
    grams[1, own] = jnp.concatenate([slab_sum(3), slab_sum(2)], axis=1)
    rhs_start(4, grams.at[1])
    rhs_wait(4, grams.at[1])
    together = grams[1]
    curvature = together[:, :count]
    curvature = 0.5 * (curvature + curvature.T)
    (alpha,) = solve_many(
        [jnp.concatenate([curvature, together[:, 128 : 128 + count]], axis=1)]
    )
    first_solution[...] += exact(alpha, all_direction[...], TN)
    all_residual[...] = all_residual[...] - exact(alpha, all_image[1], TN)
    solution_ref[...] = first_solution[own]
    residual_ref[...] = all_residual[own]


def shards(
    mesh,
    right_side,
    self_term,
    near_pairs,
    near_blocks,
    near_scale,
    near_count,
    far_pairs,
    far_left,
    far_right,
    far_scale,
    far_rank,
    far_count,
):
    n_clu, n_rhs = mesh.shape["clu"], mesh.shape["rhs"]
    rows, width = right_side.shape
    near_slots = near_blocks.shape[0]
    far_slots, rank, _ = far_left.shape
    n_cl = 2 * n_clu
    count = rows * n_rhs
    far_rows = far_slots * rank
    vmem = pl.BlockSpec(memory_space=pltpu.VMEM)
    hbm = pl.BlockSpec(memory_space=pltpu.HBM)
    field = jax.ShapeDtypeStruct((rows, width), F32)
    return pl.pallas_call(
        functools.partial(kernel, (n_clu, n_rhs, rows, near_slots, far_slots, rank)),
        out_shape=(field, field),
        in_specs=[hbm] * 12,
        out_specs=(vmem, vmem),
        scratch_shapes=[
            pltpu.VMEM((rows, width), F32),
            pltpu.VMEM((1, width), F32),
            pltpu.SMEM((2, near_slots), jnp.int32),
            pltpu.SMEM((near_slots,), F32),
            pltpu.SMEM((1,), jnp.int32),
            pltpu.SMEM((2, far_slots), jnp.int32),
            pltpu.SMEM((far_slots,), F32),
            pltpu.SMEM((far_slots,), jnp.int32),
            pltpu.SMEM((1,), jnp.int32),
            pltpu.VMEM(near_blocks.shape, BF16),
            pltpu.VMEM((far_rows, CLUSTER), BF16),
            pltpu.VMEM((far_rows, CLUSTER), BF16),
            pltpu.VMEM((1, far_rows), jnp.int32),
            pltpu.VMEM((1, far_rows), jnp.int32),
            pltpu.VMEM((1, far_rows), F32),
            pltpu.VMEM((1, far_rows), F32),
            pltpu.VMEM((n_cl * rows, far_rows), BF16),
            pltpu.VMEM((2, n_cl * rows, CLUSTER), BF16),
            pltpu.VMEM((6 * rows, CLUSTER), F32),
            pltpu.VMEM((2, n_cl * rows, CLUSTER), F32),
            pltpu.VMEM((2, n_clu, 2 * rows, CLUSTER), F32),
            pltpu.VMEM((4, n_clu, rows, 128), F32),
            pltpu.VMEM((count, width), F32),
            pltpu.VMEM((2, count, width), F32),
            pltpu.VMEM((count, width), F32),
            pltpu.VMEM((count, width), F32),
            pltpu.VMEM((2, count, 256), F32),
            pltpu.VMEM((count, width), F32),
            pltpu.SemaphoreType.DMA((9,)),
            pltpu.SemaphoreType.DMA((6,)),
            pltpu.SemaphoreType.DMA((8, n_clu)),
            pltpu.SemaphoreType.DMA((8, n_clu)),
            pltpu.SemaphoreType.DMA((5, n_rhs)),
            pltpu.SemaphoreType.DMA((5, n_rhs)),
        ],
        compiler_params=pltpu.CompilerParams(
            collective_id=0, has_side_effects=True, vmem_limit_bytes=64 * 1024 * 1024
        ),
        name="block_cg",
    )(
        right_side,
        self_term.reshape(1, width),
        near_pairs.T,
        near_scale,
        near_count,
        far_pairs.T,
        far_scale,
        far_rank,
        far_count,
        near_blocks,
        far_left.reshape(far_rows, CLUSTER),
        far_right.reshape(far_rows, CLUSTER),
    )


def solution(mesh):
    placed = (
        P("rhs", "clu"),
        P("clu"),
        P("clu", None),
        P("clu", None, None),
        P("clu"),
        P("clu"),
        P("clu", None),
        P("clu", None, None),
        P("clu", None, None),
        P("clu"),
        P("clu"),
        P("clu"),
    )
    return jax.shard_map(
        functools.partial(shards, mesh),
        mesh=mesh,
        in_specs=placed,
        out_specs=(P("rhs", "clu"), P("rhs", "clu")),
        check_vma=False,
    )
```

```python
import functools

import jax
import jax.numpy as jnp
from jax import lax
from jax.experimental import pallas as pl
from jax.experimental.pallas import tpu as pltpu
from jax.sharding import PartitionSpec as P

CLUSTER = 256
PRECISE = lax.Precision.HIGHEST
F32 = jnp.float32
BF16 = jnp.bfloat16
MESH = pl.DeviceIdType.MESH

NT = (((1,), (1,)), ((), ()))
NN = (((1,), (0,)), ((), ()))
TN = (((0,), (0,)), ((), ()))


def dot(left, right, dims):
    return lax.dot_general(left, right, dims, preferred_element_type=F32)


def exact(left, right, dims):
    return lax.dot_general(left, right, dims, precision=PRECISE, preferred_element_type=F32)


def solve_many(systems):
    size, wide = systems[0].shape
    step = 32
    row_at = lax.broadcasted_iota(jnp.int32, (size, 1), 0)

    def block(_, current):
        current = list(current)
        for k in range(0, step, 2):
            for at, m in enumerate(current):
                left = jnp.broadcast_to(m[:, k : k + 1], m.shape)
                right = jnp.broadcast_to(m[:, k + 1 : k + 2], m.shape)
                upper, lower = m[k : k + 1, :], m[k + 1 : k + 2, :]
                turn = 1.0 / left[k : k + 1, :]
                ratio = left[k + 1 : k + 2, :] * turn
                corner = right[k : k + 1, :]
                second = (lower - ratio * upper) * (
                    1.0 / (right[k + 1 : k + 2, :] - ratio * corner)
                )
                first = (upper - corner * second) * turn
                rest = m - left * first - right * second
                rest = jnp.where(row_at == k, first, rest)
                current[at] = jnp.where(row_at == k + 1, second, rest)
        return tuple(
            pltpu.roll(jnp.concatenate([m[step:], m[:step]], axis=0), wide - step, 1)
            for m in current
        )

    done = lax.fori_loop(0, size // step, block, tuple(systems))
    return [m[:, : wide - size] for m in done]


def kernel(
    sizes,
    right_hbm,
    self_hbm,
    near_pairs_hbm,
    near_scale_hbm,
    near_count_hbm,
    far_pairs_hbm,
    far_scale_hbm,
    far_rank_hbm,
    far_count_hbm,
    near_hbm,
    left_hbm,
    rightf_hbm,
    solution_ref,
    residual_ref,
    right_ref,
    self_ref,
    near_pairs,
    near_scale,
    near_count,
    far_pairs,
    far_scale,
    far_rank,
    far_count,
    near,
    far_l,
    far_r,
    meta_i,
    meta_j,
    meta_keep,
    meta_w,
    lhs,
    grid,
    around,
    sums,
    parts,
    slabs,
    all_right,
    all_image,
    all_direction,
    all_residual,
    grams,
    first_solution,
    small_sem,
    load_sem,
    clu_send,
    clu_recv,
    rhs_send,
    rhs_recv,
):
    n_clu, n_rhs, rows, near_slots, far_slots, rank = sizes
    me, col = lax.axis_index("clu"), lax.axis_index("rhs")
    n_cl = 2 * n_clu
    own = pl.ds(pl.multiple_of(col * rows, rows), rows)
    own_block = pl.ds(pl.multiple_of(me * 2 * rows, 2 * rows), 2 * rows)
    tile = 256
    slots_tile = tile // rank
    tiles = far_slots // slots_tile
    group = 2

    small = [
        pltpu.make_async_copy(src, dst, small_sem.at[k])
        for k, (src, dst) in enumerate(
            (
                (right_hbm, right_ref),
                (self_hbm, self_ref),
                (near_pairs_hbm, near_pairs),
                (near_scale_hbm, near_scale),
                (near_count_hbm, near_count),
                (far_pairs_hbm, far_pairs),
                (far_scale_hbm, far_scale),
                (far_rank_hbm, far_rank),
                (far_count_hbm, far_count),
            )
        )
    ]
    for load in small:
        load.start()

    def near_load(g):
        part = pl.ds(g * (near_slots // group), near_slots // group)
        return pltpu.make_async_copy(near_hbm.at[part], near.at[part], load_sem.at[2 + g])

    loads = [
        pltpu.make_async_copy(left_hbm, far_l, load_sem.at[0]),
        pltpu.make_async_copy(rightf_hbm, far_r, load_sem.at[1]),
    ] + [near_load(g) for g in range(group)]
    for load in loads:
        load.start()

    barrier = pltpu.get_barrier_semaphore()

    @pl.loop(1, n_clu)
    def _(d):
        pl.semaphore_signal(
            barrier, inc=1, device_id={"clu": lax.rem(me + d, n_clu)}, device_id_type=MESH
        )

    for d in range(1, n_rhs):
        pl.semaphore_signal(
            barrier, inc=1, device_id={"rhs": lax.rem(col + d, n_rhs)}, device_id_type=MESH
        )

    def clu_copy(kind, d, src, dst):
        return pltpu.make_async_remote_copy(
            src_ref=src,
            dst_ref=dst,
            send_sem=clu_send.at[kind, d],
            recv_sem=clu_recv.at[kind, d],
            device_id={"clu": lax.rem(me + d, n_clu)},
            device_id_type=MESH,
        )

    def rhs_copy(kind, d, ref):
        return pltpu.make_async_remote_copy(
            src_ref=ref.at[own],
            dst_ref=ref.at[own],
            send_sem=rhs_send.at[kind, d],
            recv_sem=rhs_recv.at[kind, d],
            device_id={"rhs": lax.rem(col + d, n_rhs)},
            device_id_type=MESH,
        )

    def rhs_start(kind, ref):
        for d in range(1, n_rhs):
            rhs_copy(kind, d, ref).start()

    def rhs_wait(kind, ref):
        for d in range(1, n_rhs):
            rhs_copy(kind, d, ref).wait()

    def grid_copy(it, d):
        block = grid.at[it, own_block]
        return clu_copy(it, d, block, block)

    def slab_copy(which, d):
        block = slabs.at[which, me]
        return clu_copy(4 + which, d, block, block)

    def sums_copy(it, d):
        there = lax.rem(me + d, n_clu)
        src = sums.at[it, pl.ds(pl.multiple_of(there * 2 * rows, 2 * rows), 2 * rows)]
        return clu_copy(2 + it, d, src, parts.at[it, me])

    def start_all(copy, which):
        @pl.loop(1, n_clu)
        def _(d):
            copy(which, d).start()

    def wait_all(copy, which):
        @pl.loop(1, n_clu)
        def _(d):
            copy(which, d).wait()

    def set_charges(it, field):
        grid[it, own_block] = jnp.concatenate(
            [field[:, :CLUSTER], field[:, CLUSTER:]], axis=0
        ).astype(BF16)

    def slab_sum(which):
        return lax.fori_loop(
            1, n_clu, lambda k, total: total + slabs[which, k], slabs[which, 0]
        )

    small[0].wait()
    field = right_ref[...]
    set_charges(0, field)
    all_right[own] = field
    pl.semaphore_wait(barrier, n_clu + n_rhs - 2)
    start_all(grid_copy, 0)
    rhs_start(0, all_right)

    for load in small[1:]:
        load.wait()

    lane = lax.broadcasted_iota(jnp.int32, (1, 128), 1)
    slot_in = lane // rank
    live = far_count[0]
    per = 128 // rank
    for g in range(far_slots // per):
        at = slice(g * 128, (g + 1) * 128)

        def spread(value):
            out = jnp.full((1, 128), value(g * per))
            for q in range(1, per):
                out = jnp.where(slot_in == q, value(g * per + q), out)
            return out

        meta_i[:, at] = spread(lambda s: far_pairs[0, s])
        meta_j[:, at] = spread(lambda s: far_pairs[1, s])
        meta_keep[:, at] = jnp.where(
            lane - slot_in * rank < spread(lambda s: far_rank[s]), 1.0, 0.0
        )
        meta_w[:, at] = spread(
            lambda s: jnp.where(s < live, far_scale[s], jnp.zeros((), F32))
        )

    rhs_wait(0, all_right)
    blank = jnp.zeros((rows, 128 - n_rhs * rows), F32)
    slabs[0, me] = jnp.concatenate([exact(all_right[own], all_right[...], NT), blank], axis=1)
    start_all(slab_copy, 0)

    def apply(it, field):
        first_far = jnp.zeros((4 * rows, CLUSTER), F32)
        for t in range(tiles):
            at = slice(t * tile, (t + 1) * tile)
            right_tile, left_tile = far_r[at, :], far_l[at, :]
            to_i, to_j = meta_i[:, at], meta_j[:, at]
            keep, weight = meta_keep[:, at], meta_w[:, at]

            def pick(b, coef):
                base = pl.multiple_of(b * 16 * rows, 16 * rows)
                product = dot(grid[it, pl.ds(base, 16 * rows)], right_tile, NT)
                for q in range(16):
                    coef = coef + jnp.where(
                        to_j == b * 16 + q, product[q * rows : (q + 1) * rows], 0.0
                    )
                return coef

            coef_second = jnp.zeros((rows, tile), F32)
            if n_cl == 16:
                coef_second = pick(0, coef_second)
            else:
                coef_second = lax.fori_loop(0, n_cl // 16, pick, coef_second)
            coef_second = jnp.where(keep > 0.0, coef_second, 0.0).astype(BF16).astype(F32) * weight
            high = coef_second.astype(BF16).astype(F32)
            low = coef_second - high
            low_cluster = to_i == 2 * me
            stack = jnp.concatenate(
                [
                    jnp.where(low_cluster, high, 0.0),
                    jnp.where(low_cluster, 0.0, high),
                    jnp.where(low_cluster, low, 0.0),
                    jnp.where(low_cluster, 0.0, low),
                ],
                axis=0,
            ).astype(BF16)
            first_far = first_far + dot(stack, left_tile, NN)
            both = dot(grid[it, own_block], left_tile, NT)
            coef_first = jnp.where(low_cluster, both[:rows], both[rows:]) * weight
            coef_first = jnp.where(keep > 0.0, coef_first, 0.0)

            def spread_rows(b, carry):
                for q in range(16):
                    base = pl.multiple_of(b * 16 * rows + q * rows, rows)
                    lhs[pl.ds(base, rows), at] = jnp.where(
                        to_j == b * 16 + q, coef_first, 0.0
                    ).astype(BF16)
                return carry

            if n_cl == 16:
                spread_rows(0, 0)
            else:
                lax.fori_loop(0, n_cl // 16, spread_rows, 0)

        def second_far(b, carry):
            part = pl.ds(pl.multiple_of(b * 16 * rows, 16 * rows), 16 * rows)
            sums[it, part] = dot(lhs[part], far_r[...], NN)
            return carry

        lax.fori_loop(0, n_cl // 16, second_far, 0)

        @pl.loop(2, n_clu - 1)
        def _(d):
            sums_copy(it, d).start()

        for side, there in enumerate((me + n_clu - 1, me, me + 1)):
            base = pl.multiple_of(lax.rem(there, n_clu) * 2 * rows, 2 * rows)
            around[side * 2 * rows : (side + 1) * 2 * rows] = grid[
                it, pl.ds(base, 2 * rows)
            ].astype(F32)
        near_live = near_count[0]
        unroll = 32
        zero = jnp.zeros((rows, CLUSTER), F32)

        def near_slots_step(g, carry):
            carry = list(carry)
            for u in range(unroll):
                s = g * unroll + u
                i, j = near_pairs[0, s], near_pairs[1, s]
                weight = jnp.where(s < near_live, near_scale[s], jnp.zeros((), F32))
                block = near[s]
                offset = j - 2 * me + 2
                offset = jnp.where(offset < 0, offset + n_cl, offset)
                offset = jnp.where(offset >= n_cl, offset - n_cl, offset)
                is_first = [jnp.where(i - 2 * me == q, 1.0, 0.0) for q in range(2)]
                is_second = [jnp.where(offset == q, 1.0, 0.0) for q in range(6)]
                first = is_first[0] * around[2 * rows : 3 * rows]
                first = first + is_first[1] * around[3 * rows : 4 * rows]
                second = is_second[0] * around[:rows]
                for q in range(1, 6):
                    second = second + is_second[q] * around[q * rows : (q + 1) * rows]
                toward_first = dot(second.astype(BF16), block, NT)
                toward_second = dot(first.astype(BF16), block, NN)
                for q in range(2):
                    carry[q] = carry[q] + (is_first[q] * weight) * toward_first
                for q in range(6):
                    carry[2 + q] = carry[2 + q] + (is_second[q] * weight) * toward_second
            return tuple(carry)

        carry = (zero,) * 8
        steps = near_slots // unroll // group
        for g in range(group):
            if it == 0:
                near_load(g).wait()
            carry = lax.fori_loop(g * steps, (g + 1) * steps, near_slots_step, carry)
        for side, there in enumerate((me + n_clu - 1, me, me + 1)):
            base = pl.multiple_of(lax.rem(there, n_clu) * 2 * rows, 2 * rows)
            pair = jnp.concatenate([carry[2 + 2 * side], carry[3 + 2 * side]], axis=0)
            if side == 1:
                pair = pair + jnp.concatenate([carry[0], carry[1]], axis=0)
                pair = pair + first_far[: 2 * rows] + first_far[2 * rows :]
            sums[it, pl.ds(base, 2 * rows)] += pair
        sums_copy(it, 1).start()
        sums_copy(it, n_clu - 1).start()
        wait_all(sums_copy, it)
        total = sums[it, own_block]

        def add(d, total):
            return total + parts[it, lax.rem(me + d, n_clu)]

        total = lax.fori_loop(1, n_clu, add, total)
        return self_ref[...] * field + jnp.concatenate([total[:rows], total[rows:]], axis=1)

    wait_all(grid_copy, 0)
    loads[0].wait()
    loads[1].wait()
    image = apply(0, field)
    all_image[0, own] = image
    rhs_start(1, all_image.at[0])
    rhs_wait(1, all_image.at[0])
    slabs[1, me] = jnp.concatenate(
        [exact(image, all_image[0], NT), exact(image, all_right[...], NT)], axis=1
    )
    start_all(slab_copy, 1)
    wait_all(slab_copy, 0)
    wait_all(slab_copy, 1)
    grams[0, own] = jnp.concatenate([slab_sum(1), slab_sum(0)], axis=1)
    rhs_start(2, grams.at[0])
    rhs_wait(2, grams.at[0])

    count = n_rhs * rows
    together = grams[0]
    image_image = together[:, :count]
    image_right = together[:, count : 2 * count]
    norms = together[:, 128 : 128 + count]
    right_image = image_right.T
    curvature = 0.5 * (image_right + right_image)
    identity = jnp.where(
        lax.broadcasted_iota(jnp.int32, (count, count), 0)
        == lax.broadcasted_iota(jnp.int32, (count, count), 1),
        1.0,
        0.0,
    )
    alpha, inverse = solve_many(
        [
            jnp.concatenate([curvature, norms], axis=1),
            jnp.concatenate([norms, identity], axis=1),
        ]
    )
    crossed = exact(right_image, alpha, NN)
    next_norms = norms - crossed - crossed.T
    next_norms = next_norms + exact(alpha, exact(image_image, alpha, NN), TN)
    beta = exact(inverse, next_norms, NN)
    all_residual[...] = all_right[...] - exact(alpha, all_image[0], TN)
    all_direction[...] = all_residual[...] + exact(beta, all_right[...], TN)
    field = all_direction[own]
    set_charges(1, field)
    start_all(grid_copy, 1)
    slabs[2, me] = jnp.concatenate(
        [exact(all_residual[own], all_residual[...], NT), blank], axis=1
    )
    start_all(slab_copy, 2)
    first_solution[...] = exact(alpha, all_right[...], TN)
    wait_all(grid_copy, 1)
    image = apply(1, field)
    all_image[1, own] = image
    rhs_start(3, all_image.at[1])
    rhs_wait(3, all_image.at[1])
    slabs[3, me] = jnp.concatenate(
        [exact(all_direction[own], all_image[1], NT), blank], axis=1
    )
    start_all(slab_copy, 3)
    wait_all(slab_copy, 2)
    wait_all(slab_copy, 3)
    grams[1, own] = jnp.concatenate([slab_sum(3), slab_sum(2)], axis=1)
    rhs_start(4, grams.at[1])
    rhs_wait(4, grams.at[1])
    together = grams[1]
    curvature = together[:, :count]
    curvature = 0.5 * (curvature + curvature.T)
    (alpha,) = solve_many(
        [jnp.concatenate([curvature, together[:, 128 : 128 + count]], axis=1)]
    )
    first_solution[...] += exact(alpha, all_direction[...], TN)
    all_residual[...] = all_residual[...] - exact(alpha, all_image[1], TN)
    solution_ref[...] = first_solution[own]
    residual_ref[...] = all_residual[own]


def shards(
    mesh,
    right_side,
    self_term,
    near_pairs,
    near_blocks,
    near_scale,
    near_count,
    far_pairs,
    far_left,
    far_right,
    far_scale,
    far_rank,
    far_count,
):
    n_clu, n_rhs = mesh.shape["clu"], mesh.shape["rhs"]
    rows, width = right_side.shape
    near_slots = near_blocks.shape[0]
    far_slots, rank, _ = far_left.shape
    n_cl = 2 * n_clu
    count = rows * n_rhs
    far_rows = far_slots * rank
    vmem = pl.BlockSpec(memory_space=pltpu.VMEM)
    hbm = pl.BlockSpec(memory_space=pltpu.HBM)
    field = jax.ShapeDtypeStruct((rows, width), F32)
    return pl.pallas_call(
        functools.partial(kernel, (n_clu, n_rhs, rows, near_slots, far_slots, rank)),
        out_shape=(field, field),
        in_specs=[hbm] * 12,
        out_specs=(vmem, vmem),
        scratch_shapes=[
            pltpu.VMEM((rows, width), F32),
            pltpu.VMEM((1, width), F32),
            pltpu.SMEM((2, near_slots), jnp.int32),
            pltpu.SMEM((near_slots,), F32),
            pltpu.SMEM((1,), jnp.int32),
            pltpu.SMEM((2, far_slots), jnp.int32),
            pltpu.SMEM((far_slots,), F32),
            pltpu.SMEM((far_slots,), jnp.int32),
            pltpu.SMEM((1,), jnp.int32),
            pltpu.VMEM(near_blocks.shape, BF16),
            pltpu.VMEM((far_rows, CLUSTER), BF16),
            pltpu.VMEM((far_rows, CLUSTER), BF16),
            pltpu.VMEM((1, far_rows), jnp.int32),
            pltpu.VMEM((1, far_rows), jnp.int32),
            pltpu.VMEM((1, far_rows), F32),
            pltpu.VMEM((1, far_rows), F32),
            pltpu.VMEM((n_cl * rows, far_rows), BF16),
            pltpu.VMEM((2, n_cl * rows, CLUSTER), BF16),
            pltpu.VMEM((6 * rows, CLUSTER), F32),
            pltpu.VMEM((2, n_cl * rows, CLUSTER), F32),
            pltpu.VMEM((2, n_clu, 2 * rows, CLUSTER), F32),
            pltpu.VMEM((4, n_clu, rows, 128), F32),
            pltpu.VMEM((count, width), F32),
            pltpu.VMEM((2, count, width), F32),
            pltpu.VMEM((count, width), F32),
            pltpu.VMEM((count, width), F32),
            pltpu.VMEM((2, count, 256), F32),
            pltpu.VMEM((count, width), F32),
            pltpu.SemaphoreType.DMA((9,)),
            pltpu.SemaphoreType.DMA((6,)),
            pltpu.SemaphoreType.DMA((8, n_clu)),
            pltpu.SemaphoreType.DMA((8, n_clu)),
            pltpu.SemaphoreType.DMA((5, n_rhs)),
            pltpu.SemaphoreType.DMA((5, n_rhs)),
        ],
        compiler_params=pltpu.CompilerParams(
            collective_id=0, has_side_effects=True, vmem_limit_bytes=64 * 1024 * 1024
        ),
        name="block_cg",
    )(
        right_side,
        self_term.reshape(1, width),
        near_pairs.T,
        near_scale,
        near_count,
        far_pairs.T,
        far_scale,
        far_rank,
        far_count,
        near_blocks,
        far_left.reshape(far_rows, CLUSTER),
        far_right.reshape(far_rows, CLUSTER),
    )


def solution(mesh):
    placed = (
        P("rhs", "clu"),
        P("clu"),
        P("clu", None),
        P("clu", None, None),
        P("clu"),
        P("clu"),
        P("clu", None),
        P("clu", None, None),
        P("clu", None, None),
        P("clu"),
        P("clu"),
        P("clu"),
    )
    return jax.shard_map(
        functools.partial(shards, mesh),
        mesh=mesh,
        in_specs=placed,
        out_specs=(P("rhs", "clu"), P("rhs", "clu")),
        check_vma=False,
    )
```
